256 devices in a mesh: dp: 4 (over z_lo), feat: 64 (over y, z_hi, x, core).
Axes of the slice: x: 4, y: 4, z: 8 (z_hi: 2, z_lo: 4; z = z_hi * 4 + z_lo), core: 2. Of those that a mesh axis runs over, the one named last changes fastest.
Arguments:
- features: bfloat16 [1024, 32768], P('dp', 'feat'), may hold values from -6 to 6
- diag_first: bfloat16 [128, 256, 256], P('feat'), may hold values from -0.125 to 0.125
- part_first: bfloat16 [7, 128, 256, 256], P(None, 'feat'), may hold values from -0.125 to 0.125
- bias_first: bfloat16 [32768], P('feat'), may hold values from -3 to 3
- diag_second: bfloat16 [128, 256, 256], P('feat'), may hold values from -0.125 to 0.125
- part_second: bfloat16 [7, 128, 256, 256], P(None, 'feat'), may hold values from -0.125 to 0.125
- section_bit: int32 [7], replicated, may hold values from 0 to 6, each once
- grad_out: bfloat16 [1024, 32768], P('dp', 'feat'), may hold values from -6 to 6
Outputs:
- output: bfloat16 [1024, 32768], P('dp', 'feat')
- grad_features: bfloat16 [1024, 32768], P('dp', 'feat')
- grad_diag_first: bfloat16 [128, 256, 256], P('feat')
- grad_part_first: bfloat16 [7, 128, 256, 256], P(None, 'feat')
- grad_bias_first: bfloat16 [32768], P('feat')
- grad_diag_second: bfloat16 [128, 256, 256], P('feat')
- grad_part_second: bfloat16 [7, 128, 256, 256], P(None, 'feat')
The draws below stay inside these ranges and needn't reach their ends.
Inputs may be any that keep to these rules, and one draw needn't show every extreme that they name: section_bit holds each of 0 to 6 exactly once.
All inputs are finite; a program needn't handle non-finite values.
Results may differ from the reference program's by a relative error of at most 0.019.
Values may be sent and summed in bfloat16 or wider, within the bound.
No kernel may reach another device: no remote copies, remote signals or barrier semaphores. Data moves between devices by JAX's collectives and lax.ppermute only.
A program may use at most 64 MiB of HBM per device.

```python
import jax
import jax.numpy as jnp
from jax import lax

SECTIONS = 7
BS = 256
NB = 128
F = 32768
TOK_DEV = 256
ROWS = 1024
N_DP = 4


def shard_levels(own_key, extent, shards, smallest, largest):
    gain, own = 1.0, jax.random.fold_in(own_key, 6)
    for position, blocks in shards:
        heights = jnp.exp(jax.random.uniform(jax.random.fold_in(own, position), (blocks,), jnp.float32, smallest / len(shards), largest / len(shards)))
        gain = gain * jnp.repeat(heights, extent[position] // blocks).reshape([-1 if axis == position else 1 for axis in range(len(extent))])
    return gain


def noise(key, shape, deviation, reach, shards=(), held_as=jnp.bfloat16):
    array = jax.random.normal(key, shape, jnp.float32) * deviation
    if len(shards) > 0:
        array = shard_levels(key, shape, shards, -0.22, 0.18) * array
    return jnp.clip(array, min=-reach, max=reach).astype(held_as)


def setup_inputs(seed: int = 0) -> dict:
    seeds = jax.random.split(jax.random.key(seed), 9)
    return {
        "features": noise(seeds[0], (ROWS, F), 1.0, 6.0, ((0, 4), (1, 64))),
        "diag_first": noise(seeds[1], (NB, BS, BS), ((SECTIONS + 1) * BS) ** -0.5, 0.125, ((0, 64),)),
        "part_first": noise(seeds[2], (SECTIONS, NB, BS, BS), ((SECTIONS + 1) * BS) ** -0.5, 0.125, ((1, 64),)),
        "bias_first": noise(seeds[3], (F,), 0.5, 3.0, ((0, 64),)),
        "diag_second": noise(seeds[4], (NB, BS, BS), ((SECTIONS + 1) * BS) ** -0.5, 0.125, ((0, 64),)),
        "part_second": noise(seeds[5], (SECTIONS, NB, BS, BS), ((SECTIONS + 1) * BS) ** -0.5, 0.125, ((1, 64),)),
        "section_bit": jax.random.permutation(seeds[6], SECTIONS).astype(jnp.int32),
        "grad_out": noise(seeds[7], (ROWS, F), 1.0, 6.0, ((0, 4), (1, 64))),
    }


def partner_index(level):
    shifted = jnp.left_shift(jnp.int32(1), level.astype(jnp.int32)).astype(jnp.int32)
    return jnp.bitwise_xor(jnp.arange(NB, dtype=jnp.int32), shifted).astype(jnp.int32)

def as_float(value):
    return value.astype(jnp.float32)

def forward_mix(blocks, diagonal, partner, section_bit):
    total = jnp.einsum('rib,ibc->ric', as_float(blocks), as_float(diagonal))
    for section in range(SECTIONS):
        other = jnp.take(blocks, partner_index(section_bit[section]), axis=1)
        total = total + jnp.einsum('rib,ibc->ric', as_float(other), as_float(partner[section]))
    return total

def backward_mix(grad, diagonal, partner, section_bit):
    total = jnp.einsum('ric,ibc->rib', as_float(grad), as_float(diagonal))
    for section in range(SECTIONS):
        product_term = jnp.einsum('ric,ibc->rib', as_float(grad), as_float(partner[section]))
        total = total + jnp.take(product_term, partner_index(section_bit[section]), axis=1)
    return total

def settle(partial_value):
    rounded = lax.optimization_barrier(partial_value.astype(jnp.bfloat16))
    return lax.optimization_barrier(jnp.sum(rounded.astype(jnp.float32), axis=0)).astype(jnp.bfloat16)

def weight_sums(blocks, grad, section_bit):
    grouped_in = as_float(blocks).reshape(N_DP, TOK_DEV, NB, BS)
    grouped_grad = as_float(grad).reshape(N_DP, TOK_DEV, NB, BS)
    diag_grad = settle(jnp.einsum('grib,gric->gibc', grouped_in, grouped_grad))
    pieces = []
    for section in range(SECTIONS):
        other = jnp.take(grouped_in, partner_index(section_bit[section]), axis=2)
        pieces.append(settle(jnp.einsum('grib,gric->gibc', other, grouped_grad)))
    return (diag_grad, jnp.stack(pieces))

def reference(features, diag_first, part_first, bias_first, diag_second, part_second, section_bit, grad_out):
    blocks = features.reshape(ROWS, NB, BS)
    pre = forward_mix(blocks, diag_first, part_first, section_bit) + as_float(bias_first).reshape(NB, BS)
    hidden = jax.nn.gelu(pre, approximate=True).astype(jnp.bfloat16)
    output = forward_mix(hidden, diag_second, part_second, section_bit).astype(jnp.bfloat16)
    grad_blocks = grad_out.reshape(ROWS, NB, BS)
    grad_hidden = backward_mix(grad_blocks, diag_second, part_second, section_bit)
    _, pull = jax.vjp(lambda value: jax.nn.gelu(value, approximate=True), pre)
    grad_pre = pull(grad_hidden)[0].astype(jnp.bfloat16)
    grad_in = backward_mix(grad_pre, diag_first, part_first, section_bit).astype(jnp.bfloat16)
    grad_diag_two, grad_part_two = weight_sums(hidden, grad_blocks, section_bit)
    grad_diag_one, grad_part_one = weight_sums(blocks, grad_pre, section_bit)
    grad_bias = settle(lax.optimization_barrier(jnp.sum(as_float(grad_pre).reshape(N_DP, TOK_DEV, F), axis=1)))
    return (output.reshape(ROWS, F), grad_in.reshape(ROWS, F), grad_diag_one, grad_part_one, grad_bias, grad_diag_two, grad_part_two)
```

```python
import jax
import jax.numpy as jnp
from jax import lax
from jax.experimental import pallas as pl
from jax.experimental.pallas import tpu as pltpu
from jax.sharding import PartitionSpec as P

SECTIONS = 7
BS = 256
COLS = 512
ROWS = 256
N_DP = 4
N_FEAT = 64
CORE, X1, X2, ZHI, Y1, Y2 = range(6)
DEVICE_BITS = 6
SQRT_2_OVER_PI = 0.7978845608028654
CUBIC = 0.044715
VMEM_LIMIT = 48 * 1024 * 1024
BF16 = jnp.bfloat16
F32 = jnp.float32


def from_partner(value, bit):
    pairs = [(source, source ^ (1 << bit)) for source in range(N_FEAT)]
    return lax.ppermute(value, "feat", pairs)


def along_z(value, step):
    pairs = []
    for dp in range(N_DP):
        for feat in range(N_FEAT):
            z_hi = (feat >> 3) & 1
            z = (z_hi * N_DP + dp + step) % (2 * N_DP)
            to_feat = (feat & ~8) | ((z // N_DP) << 3)
            pairs.append((dp * N_FEAT + feat, (z % N_DP) * N_FEAT + to_feat))
    return lax.ppermute(value, ("dp", "feat"), pairs)


def gather_z(value):
    up, down, ups, downs = value, value, [], []
    for _ in range(3):
        up, down = along_z(up, 1), along_z(down, -1)
        ups.append(up)
        downs.append(down)
    return ups, downs


def line_rows(ups, downs, dp):
    first = jnp.where(dp == 3, ups[0], downs[0])
    second = jnp.where(dp <= 1, downs[1], ups[1])
    third = jnp.where(dp == 0, downs[2], jnp.where(dp == 3, ups[2], ups[0]))
    return [first, second, third]


def far_rows(ups, downs, dp):
    first = jnp.where(dp == 3, downs[2], ups[2])
    second = jnp.where(dp <= 1, ups[1], downs[1])
    third = jnp.where(dp == 0, ups[0], jnp.where(dp == 3, downs[0], downs[2]))
    return [first, second, third]


def dot(a, b):
    return jnp.dot(a, b, preferred_element_type=F32)


def dot_t(a, b):
    return lax.dot_general(a, b, (((1,), (1,)), ((), ())), preferred_element_type=F32)


def t_dot(a, b):
    return lax.dot_general(a, b, (((0,), (0,)), ((), ())), preferred_element_type=F32)


def half(block):
    return slice(block * BS, (block + 1) * BS)


def gelu_parts(value):
    inner = SQRT_2_OVER_PI * (value + CUBIC * value * value * value)
    return jnp.tanh(inner)


def mix_block(order, own, others, diag, part, block):
    total = dot(own[:, half(block)], diag[block])
    total = total + dot(own[:, half(1 - block)], part[order[0], block])
    for bit in range(DEVICE_BITS):
        total = total + dot(others[bit][:, half(block)], part[order[bit + 1], block])
    return total


def forward_kernel(order, own, *refs):
    others, (diag, part, bias, pre_out, hidden_out) = refs[:6], refs[6:]
    for block in range(2):
        pre = mix_block(order, own, others, diag, part, block)
        pre = pre + bias[:, half(block)].astype(F32)
        pre_out[:, half(block)] = pre
        hidden_out[:, half(block)] = (0.5 * pre * (1.0 + gelu_parts(pre))).astype(BF16)


def output_kernel(order, own, *refs):
    others, (diag, part, out) = refs[:6], refs[6:]
    for block in range(2):
        out[:, half(block)] = mix_block(order, own, others, diag, part, block).astype(BF16)


def products(order, grad, diag, part, local, sent):
    for block in range(2):
        value = grad[:, half(block)]
        other = grad[:, half(1 - block)]
        local[:, half(block)] = dot_t(value, diag[block]) + dot_t(other, part[order[0], 1 - block])
        for bit in range(DEVICE_BITS):
            sent[bit][:, half(block)] = dot_t(value, part[order[bit + 1], block]).astype(BF16)


def products_kernel(order, grad, diag, part, local, *sent):
    products(order, grad, diag, part, local, sent)


def grad_pre_kernel(order, pre, local_in, *refs):
    got, (diag, part, grad_pre, local, *sent) = refs[:6], refs[6:]
    for block in range(2):
        total = local_in[:, half(block)]
        for bit in range(DEVICE_BITS):
            total = total + got[bit][:, half(block)].astype(F32)
        value = pre[:, half(block)]
        tanh = gelu_parts(value)
        slope = SQRT_2_OVER_PI * (1.0 + (3.0 * CUBIC) * value * value)
        gain = 0.5 * (1.0 + tanh) + 0.5 * value * (1.0 - tanh * tanh) * slope
        grad_pre[:, half(block)] = (total * gain).astype(BF16)
    products(order, grad_pre, diag, part, local, sent)


def sum_kernel(local_in, *refs):
    got, out = refs[:6], refs[6]
    total = local_in[...]
    for bit in range(DEVICE_BITS):
        total = total + got[bit][...].astype(F32)
    out[...] = total.astype(BF16)


def weight_kernel(order, *refs):
    own, far, grad = refs[0:4], refs[4:8], refs[8:12]
    near, near_rest = refs[12:17], refs[17:22]
    diag_out, part_out, bias_out = refs[22:25]
    for block in range(2):
        grads = jnp.concatenate([ref[:, half(block)] for ref in grad], axis=0)
        stacked = [jnp.concatenate([ref[:, half(b)] for ref in own], axis=0) for b in range(2)]
        diag_out[block] = t_dot(stacked[block], grads).astype(BF16)
        part_out[order[0], block] = t_dot(stacked[1 - block], grads).astype(BF16)
        value = jnp.concatenate([ref[:, half(block)] for ref in far], axis=0)
        part_out[order[ZHI + 1], block] = t_dot(value, grads).astype(BF16)
        for at, bit in enumerate((CORE, X1, X2, Y1, Y2)):
            value = jnp.concatenate(
                [near[at][:, half(block)], near_rest[at][:, half(block)]], axis=0
            )
            part_out[order[bit + 1], block] = t_dot(value, grads).astype(BF16)
        bias_out[:, half(block)] = jnp.sum(grads.astype(F32), axis=0, keepdims=True).astype(BF16)


def shape(rows, dtype):
    return jax.ShapeDtypeStruct((rows, COLS), dtype)


WEIGHTS = (
    jax.ShapeDtypeStruct((2, BS, BS), BF16),
    jax.ShapeDtypeStruct((SECTIONS, 2, BS, BS), BF16),
)


def call(kernel, name, out_shape, flops, args, order=None):
    vmem = pl.BlockSpec(memory_space=pltpu.VMEM)
    specs = [vmem] * len(args)
    if order is not None:
        specs = [pl.BlockSpec(memory_space=pltpu.SMEM)] + specs
        args = (order, *args)
    moved = sum(a.size * a.dtype.itemsize for a in (*args, *out_shape))
    return pl.pallas_call(
        kernel,
        out_shape=out_shape,
        in_specs=specs,
        out_specs=[vmem] * len(out_shape),
        compiler_params=pltpu.CompilerParams(vmem_limit_bytes=VMEM_LIMIT),
        cost_estimate=pl.CostEstimate(flops=flops, bytes_accessed=moved, transcendentals=0),
        name=name,
    )(*args)


MAP_FLOPS = 2 * 16 * BS * BS * BS


def on_device(
    features, diag_first, part_first, bias_first, diag_second, part_second, section_bit, grad_out
):
    dp = lax.axis_index("dp")
    order = jnp.sum(
        jnp.where(
            section_bit[None, :] == jnp.arange(SECTIONS, dtype=jnp.int32)[:, None],
            jnp.arange(SECTIONS, dtype=jnp.int32)[None, :],
            0,
        ),
        axis=1,
    )
    near_bits = (CORE, X1, X2, Y1, Y2)
    bits = range(DEVICE_BITS)

    others = [from_partner(features, bit) for bit in bits]
    local_second, *sent = call(
        products_kernel,
        "products_second",
        (shape(ROWS, F32), *[shape(ROWS, BF16)] * 6),
        MAP_FLOPS,
        (grad_out, diag_second, part_second),
        order,
    )
    got = [from_partner(sent[bit], bit) for bit in bits]
    pre, hidden = call(
        forward_kernel,
        "forward_first",
        (shape(ROWS, F32), shape(ROWS, BF16)),
        MAP_FLOPS,
        (features, *others, diag_first, part_first, bias_first.reshape(1, COLS)),
        order,
    )
    early_up, early_down = gather_z(jnp.concatenate([features, grad_out], axis=0))
    hidden_up, hidden_down = gather_z(hidden)
    hidden_others = [from_partner(hidden, bit) for bit in bits]
    grad_pre, local_first, *sent = call(
        grad_pre_kernel,
        "grad_pre",
        (shape(ROWS, BF16), shape(ROWS, F32), *[shape(ROWS, BF16)] * 6),
        MAP_FLOPS,
        (pre, local_second, *got, diag_first, part_first),
        order,
    )
    got_first = [from_partner(sent[bit], bit) for bit in bits]
    pre_up, pre_down = gather_z(grad_pre)

    early_rows = line_rows(early_up, early_down, dp)
    feature_rows = [value[:ROWS] for value in early_rows]
    out_rows = [value[ROWS:] for value in early_rows]
    feature_far = [value[:ROWS] for value in far_rows(early_up, early_down, dp)]
    stacked = jnp.concatenate(feature_rows, axis=0)
    feature_near = [from_partner(stacked, bit) for bit in near_bits]
    hidden_rows = line_rows(hidden_up, hidden_down, dp)
    hidden_far = far_rows(hidden_up, hidden_down, dp)
    stacked = jnp.concatenate(hidden_rows, axis=0)
    hidden_near = [from_partner(stacked, bit) for bit in near_bits]
    pre_rows = line_rows(pre_up, pre_down, dp)

    (output,) = call(
        output_kernel,
        "forward_second",
        (shape(ROWS, BF16),),
        MAP_FLOPS,
        (hidden, *hidden_others, diag_second, part_second),
        order,
    )
    (grad_in,) = call(
        sum_kernel, "grad_features", (shape(ROWS, BF16),), 0, (local_first, *got_first)
    )
    diag_first_grad, part_first_grad, bias_grad = call(
        weight_kernel,
        "weights_first",
        (*WEIGHTS, shape(1, BF16)),
        N_DP * MAP_FLOPS,
        (
            features,
            *feature_rows,
            others[ZHI],
            *feature_far,
            grad_pre,
            *pre_rows,
            *[others[bit] for bit in near_bits],
            *feature_near,
        ),
        order,
    )
    diag_second_grad, part_second_grad, _ = call(
        weight_kernel,
        "weights_second",
        (*WEIGHTS, shape(1, BF16)),
        N_DP * MAP_FLOPS,
        (
            hidden,
            *hidden_rows,
            hidden_others[ZHI],
            *hidden_far,
            grad_out,
            *out_rows,
            *[hidden_others[bit] for bit in near_bits],
            *hidden_near,
        ),
        order,
    )
    return (
        output,
        grad_in,
        diag_first_grad,
        part_first_grad,
        bias_grad.reshape(COLS),
        diag_second_grad,
        part_second_grad,
    )


def solution(mesh):
    in_specs = (
        P("dp", "feat"),
        P("feat", None, None),
        P(None, "feat", None, None),
        P("feat"),
        P("feat", None, None),
        P(None, "feat", None, None),
        P(),
        P("dp", "feat"),
    )
    out_specs = (
        P("dp", "feat"),
        P("dp", "feat"),
        P("feat", None, None),
        P(None, "feat", None, None),
        P("feat"),
        P("feat", None, None),
        P(None, "feat", None, None),
    )
    return jax.shard_map(
        on_device, mesh=mesh, in_specs=in_specs, out_specs=out_specs, check_vma=False
    )
```

```python
import jax
import jax.numpy as jnp
from jax import lax
from jax.experimental import pallas as pl
from jax.experimental.pallas import tpu as pltpu
from jax.sharding import PartitionSpec as P

SECTIONS = 7
BS = 256
COLS = 512
ROWS = 256
REST = 768
N_DP = 4
N_FEAT = 64
CORE, X1, X2, ZHI, Y1, Y2 = range(6)
DEVICE_BITS = 6
FEAT = ("y", "z_hi", "x_core")
NEAR = (CORE, X1, X2, Y1, Y2)
START_ORDER = (ZHI, X2, Y2, CORE, X1, Y1)
SQRT_2_OVER_PI = 0.7978845608028654
CUBIC = 0.044715
VMEM_LIMIT = 60 * 1024 * 1024
BF16 = jnp.bfloat16
F32 = jnp.float32


def after(*values):
    return lax.optimization_barrier(values)


def from_partner(value, bit):
    pairs = [(source, source ^ (1 << bit)) for source in range(N_FEAT)]
    return lax.ppermute(value, FEAT, pairs)


def send(values):
    return {bit: from_partner(value, bit) for bit, value in values.items()}


def join(arrived, *values):
    tied = after(*arrived.values(), *values)
    return dict(zip(arrived, tied)), tied[len(arrived) :]


def tie(pair, *values):
    tied = after(*pair, *values)
    return tied[:2], tied[2:]


def along_z(value, step):
    pairs = []
    for dp in range(N_DP):
        for feat in range(N_FEAT):
            z_hi = (feat >> 3) & 1
            z = (z_hi * N_DP + dp + step) % (2 * N_DP)
            to_feat = (feat & ~8) | ((z // N_DP) << 3)
            pairs.append((dp * N_FEAT + feat, (z % N_DP) * N_FEAT + to_feat))
    return lax.ppermute(value, ("dp", *FEAT), pairs)


def both_ways(up, down):
    return along_z(up, 1), along_z(down, -1)


LINE = (
    ((1, 0), (1, 1), (1, 2)),
    ((1, 0), (1, 1), (0, 0)),
    ((1, 0), (0, 1), (0, 0)),
    ((0, 0), (0, 1), (0, 2)),
)
FAR = (
    ((0, 2), (0, 1), (0, 0)),
    ((0, 2), (0, 1), (1, 2)),
    ((0, 2), (1, 1), (1, 2)),
    ((1, 2), (1, 1), (1, 0)),
)


def dot(a, b):
    return jnp.dot(a, b, preferred_element_type=F32)


def dot_t(a, b):
    return lax.dot_general(a, b, (((1,), (1,)), ((), ())), preferred_element_type=F32)


def t_dot(a, b):
    return lax.dot_general(a, b, (((0,), (0,)), ((), ())), preferred_element_type=F32)


def sections_of(bits):
    return [
        sum(jnp.where(bits[section] == level, section, 0) for section in range(SECTIONS))
        for level in range(SECTIONS)
    ]


def half(block):
    return slice(block * BS, (block + 1) * BS)


def mix_block(order, own, others, diag, part, block):
    total = dot(own[0:ROWS, half(block)], diag[block])
    total = total + dot(own[0:ROWS, half(1 - block)], part[order[0], block])
    for bit in range(DEVICE_BITS):
        total = total + dot(others[bit][0:ROWS, half(block)], part[order[bit + 1], block])
    return total


def products(order, grad, diag, part, local, sent):
    for block in range(2):
        value = grad[:, half(block)]
        other = grad[:, half(1 - block)]
        local[:, half(block)] = dot_t(value, diag[block]) + dot_t(other, part[order[0], 1 - block])
        for bit in range(DEVICE_BITS):
            term = dot_t(value, part[order[bit + 1], block]).astype(BF16)
            sent[bit][sent[bit].shape[0] - ROWS :, half(block)] = term


def first_kernel(bits, features, grad, diag, part, local, *sent):
    order = sections_of(bits)
    for bit in range(DEVICE_BITS):
        sent[bit][0:ROWS] = features[...]
    products(order, grad, diag, part, local, sent)


def middle_kernel(bits, features, local_in, *refs):
    got, (diag, part, bias, late, local, *sent) = refs[:6], refs[6:]
    order = sections_of(bits)
    for block in range(2):
        pre = mix_block(order, features, got, diag, part, block)
        pre = pre + bias[half(block)].astype(F32)[None, :]
        tanh = jnp.tanh(SQRT_2_OVER_PI * (pre + CUBIC * pre * pre * pre))
        hidden = (0.5 * pre * (1.0 + tanh)).astype(BF16)
        late[0:ROWS, half(block)] = hidden
        for bit in NEAR:
            sent[bit][0:ROWS, half(block)] = hidden
        total = local_in[:, half(block)]
        for bit in range(DEVICE_BITS):
            total = total + got[bit][ROWS:, half(block)].astype(F32)
        slope = SQRT_2_OVER_PI * (1.0 + (3.0 * CUBIC) * pre * pre)
        gain = 0.5 * (1.0 + tanh) + 0.5 * pre * (1.0 - tanh * tanh) * slope
        late[ROWS : 2 * ROWS, half(block)] = (total * gain).astype(BF16)
    products(order, late.at[ROWS : 2 * ROWS], diag, part, local, sent)


def last_kernel(bits, hidden, *refs):
    order = sections_of(bits)
    got, got_far, far, (local, diag, part, out, grad_in) = refs[:5], refs[5], refs[6], refs[7:]
    others = dict(zip(NEAR, got))
    others[ZHI] = far
    for block in range(2):
        total = mix_block(order, hidden, others, diag, part, block)
        out[:, half(block)] = total.astype(BF16)
    total = local[...] + got_far[...].astype(F32)
    for ref in got:
        total = total + ref[ROWS:].astype(F32)
    grad_in[...] = total.astype(BF16)


def of_this_dp(body):
    for dp in range(N_DP):

        @pl.when(lax.axis_index("dp") == dp)
        def _():
            body(dp)


def rows_kernel(bits, *refs):
    chunks, out, sem = (refs[0:3], refs[3:6]), refs[6], refs[7]

    def copy(way, step, at):
        return pltpu.make_async_copy(
            chunks[way][step].at[pl.ds(0, ROWS)], out.at[pl.ds(at * ROWS, ROWS)], sem.at[at]
        )

    @of_this_dp
    def _(dp):
        for at, (way, step) in enumerate(LINE[dp]):
            copy(way, step, at).start()

    for at in range(3):
        copy(0, 0, at).wait()


def other_dp(dp, at):
    way, step = LINE[dp][at]
    return dp + 1 + step if way else dp - 1 - step


def gathered_row(dp, far, rows):
    z_hi = lax.axis_index("z_hi")
    if far:
        z_hi = 1 - z_hi
    return pl.multiple_of((z_hi * N_DP + dp) * rows, rows)


def hidden_rows_kernel(bits, gathered, rows, far, sem):
    def copy(row, out, at, order):
        return pltpu.make_async_copy(
            gathered.at[pl.ds(row, ROWS)], out.at[pl.ds(at * ROWS, ROWS)], sem.at[order]
        )

    @of_this_dp
    def _(dp):
        for at in range(3):
            copy(gathered_row(other_dp(dp, at), False, 2 * ROWS), rows, at, at).start()
        copy(gathered_row(dp, True, 2 * ROWS), far, 0, 3).start()

    for at in range(3):
        copy(0, rows, at, at).wait()
    copy(0, far, 0, 3).wait()


def weight_kernel(second, bits, *refs):
    order = sections_of(bits)
    own, own_rest, far, grad, gathered = refs[0:5]
    near, near_rest = refs[5:10], refs[10:15]
    chunks = (refs[15:18], refs[18:21])
    diag_out, part_out, bias_out, own_buf, far_buf, grad_buf, near_buf, sems = refs[21:]

    def copy(source, at, rows, target, to, sem):
        return pltpu.make_async_copy(
            source.at[pl.ds(at, rows)], target.at[pl.ds(to, rows)], sems.at[sem]
        )

    def grad_copy(at, source, row):
        return copy(source, row, ROWS, grad_buf, (at + 1) * ROWS, 1 + at)

    def far_copy(at, source, row):
        return copy(source, row, ROWS, far_buf, (at + 1) * ROWS, 7 + at)

    grad_copies = [copy(grad, 0 if second else ROWS, ROWS, grad_buf, 0, 0)]
    grad_copies += [grad_copy(at, gathered, 0) for at in range(3)]
    far_copies = [copy(far, 0, ROWS, far_buf, 0, 6)]
    far_copies += [far_copy(at, gathered, 0) for at in range(3)]
    own_copies = [
        copy(own, 0, ROWS, own_buf, 0, 4),
        copy(own_rest, 0, REST, own_buf, ROWS, 5),
    ]
    near_copies = []
    for at in range(5):
        buf = near_buf.at[at]
        near_copies.append(
            [
                copy(near[at], 0, ROWS, buf, 0, 10 + 2 * at),
                copy(near_rest[at], 0, REST, buf, ROWS, 11 + 2 * at),
            ]
        )
    grad_copies[0].start()

    @of_this_dp
    def _(dp):
        for at in range(3):
            other = other_dp(dp, at)
            if second:
                way, step = LINE[dp][at]
                source = chunks[way][step]
                grad_copy(at, source, source.shape[0] - ROWS).start()
                far_copy(at, gathered, gathered_row(other, True, 2 * ROWS)).start()
            else:
                row = gathered_row(other, False, 2 * ROWS)
                grad_copy(at, gathered, row + ROWS).start()
                way, step = FAR[dp][at]
                far_copy(at, chunks[way][step], 0).start()

    for item in (*own_copies, far_copies[0]):
        item.start()
    for pair in near_copies:
        for item in pair:
            item.start()
    for item in grad_copies:
        item.wait()
    for block in range(2):
        total = jnp.sum(grad_buf[:, half(block)].astype(F32), axis=0, keepdims=True)
        bias_out[half(block)] = total[0].astype(BF16)
    for item in own_copies:
        item.wait()
    for block in range(2):
        grads = grad_buf[:, half(block)]
        diag_out[block] = t_dot(own_buf[:, half(block)], grads).astype(BF16)
        part_out[order[0], block] = t_dot(own_buf[:, half(1 - block)], grads).astype(BF16)
    for item in far_copies:
        item.wait()
    for block in range(2):
        term = t_dot(far_buf[:, half(block)], grad_buf[:, half(block)])
        part_out[order[ZHI + 1], block] = term.astype(BF16)
    for at, bit in enumerate(NEAR):
        for item in near_copies[at]:
            item.wait()
        for block in range(2):
            term = t_dot(near_buf[at, :, half(block)], grad_buf[:, half(block)])
            part_out[order[bit + 1], block] = term.astype(BF16)


def shape(rows, dtype=BF16):
    return jax.ShapeDtypeStruct((rows, COLS), dtype)


def whole(value):
    zeros = (0,) * len(value.shape)
    return pl.BlockSpec(value.shape, lambda step: zeros)


HBM = pl.BlockSpec(memory_space=pl.ANY)
SCALARS = pl.BlockSpec(memory_space=pltpu.SMEM)
MAP_FLOPS = 2 * 16 * BS * BS * BS


def call(kernel, name, out_shape, flops, bits, args, fetch=True, scratch=(), outs=None):
    moved = sum(a.size * a.dtype.itemsize for a in (*args, *out_shape))
    return pl.pallas_call(
        kernel,
        grid=(1,),
        out_shape=out_shape,
        in_specs=[SCALARS] + [whole(value) if fetch else HBM for value in args],
        out_specs=outs or [whole(value) for value in out_shape],
        scratch_shapes=scratch,
        compiler_params=pltpu.CompilerParams(vmem_limit_bytes=VMEM_LIMIT),
        cost_estimate=pl.CostEstimate(flops=flops, bytes_accessed=moved, transcendentals=0),
        name=name,
    )(bits, *args)


def chunks_of(steps):
    return [item[0] for item in steps] + [item[1] for item in steps]


def rows_of_line(name, bits, steps):
    (rows,) = call(
        rows_kernel,
        name,
        (shape(REST),),
        0,
        bits,
        chunks_of(steps),
        fetch=False,
        scratch=[pltpu.SemaphoreType.DMA((3,))],
    )
    return rows


def weight_sums(name, bits, second, args):
    def kernel(*refs):
        weight_kernel(second, *refs)

    stacked = (N_DP * ROWS, COLS)
    return call(
        kernel,
        name,
        (
            jax.ShapeDtypeStruct((2, BS, BS), BF16),
            jax.ShapeDtypeStruct((SECTIONS, 2, BS, BS), BF16),
            jax.ShapeDtypeStruct((COLS,), BF16),
        ),
        N_DP * MAP_FLOPS,
        bits,
        args,
        fetch=False,
        scratch=[
            pltpu.VMEM(stacked, BF16),
            pltpu.VMEM(stacked, BF16),
            pltpu.VMEM(stacked, BF16),
            pltpu.VMEM((5, *stacked), BF16),
            pltpu.SemaphoreType.DMA((20,)),
        ],
    )


def on_device(
    features, diag_first, part_first, bias_first, diag_second, part_second, section_bit, grad_out
):
    bits = range(DEVICE_BITS)

    features_z = [both_ways(features, features)]
    local_second, *sent = call(
        first_kernel,
        "products_second",
        (shape(ROWS, F32), *[shape(2 * ROWS)] * 6),
        MAP_FLOPS,
        section_bit,
        (features, grad_out, diag_second, part_second),
    )
    *ends, local_second = after(*features_z[0], *sent, local_second)
    sent = ends[2:]
    got = send({bit: sent[bit] for bit in START_ORDER})
    up, down, *tied = after(*ends[:2], *[got[bit] for bit in bits])
    got = dict(zip(bits, tied))
    features_z[0] = (up, down)
    features_z.append(
        both_ways(*[jnp.concatenate([value, grad_out], axis=0) for value in (up, down)])
    )
    late, local_first, *sent = call(
        middle_kernel,
        "hidden_and_grad_pre",
        (shape(2 * ROWS), shape(ROWS, F32))
        + tuple(shape(ROWS if bit == ZHI else 2 * ROWS) for bit in bits),
        2 * MAP_FLOPS,
        section_bit,
        (
            features,
            local_second,
            *[got[bit] for bit in bits],
            diag_first,
            part_first,
            bias_first,
        ),
    )
    up, down, late = after(*features_z[1], late)
    features_z[1] = (up, down)
    gathered = lax.all_gather(late, ("z_hi", "dp"), axis=0, tiled=True)
    features_z.append(both_ways(up, down))
    got_late = send({bit: sent[bit] for bit in (X2, Y2, X1)})
    features_z[2], (sent[Y1], sent[CORE]) = tie(features_z[2], sent[Y1], sent[CORE])
    got_late.update(send({Y1: sent[Y1], CORE: sent[CORE]}))
    feature_rows = rows_of_line("feature_rows", section_bit, features_z)
    feature_rows, got_late[X2], got_late[Y2] = after(feature_rows, got_late[X2], got_late[Y2])
    feature_near = send({X2: feature_rows, Y2: feature_rows})
    got_late, (feature_rows,) = join(got_late, feature_rows)
    feature_near.update(send({X1: feature_rows, Y1: feature_rows, CORE: feature_rows}))
    gathered, feature_near[X2], feature_near[Y2] = after(
        gathered, feature_near[X2], feature_near[Y2]
    )
    hidden_rows, hidden_far = call(
        hidden_rows_kernel,
        "hidden_rows",
        (shape(REST), shape(ROWS)),
        0,
        section_bit,
        (gathered,),
        fetch=False,
        scratch=[pltpu.SemaphoreType.DMA((4,))],
    )
    hidden_near = send({X2: hidden_rows, Y2: hidden_rows})
    feature_near, (hidden_rows,) = join(feature_near, hidden_rows)
    hidden_near.update(send({X1: hidden_rows, Y1: hidden_rows, CORE: hidden_rows}))
    far_product, hidden_near[CORE] = after(sent[ZHI], hidden_near[CORE])
    got_late[ZHI] = from_partner(far_product, ZHI)
    up, down, hidden_near[X2], hidden_near[Y2] = after(
        *features_z[2], hidden_near[X2], hidden_near[Y2]
    )
    grad_z = [*features_z[1:], both_ways(up[ROWS:], down[ROWS:])]
    diag_first_grad, part_first_grad, bias_grad = weight_sums(
        "weights_first",
        section_bit,
        False,
        (
            features,
            feature_rows,
            got[ZHI],
            late,
            gathered,
            *[got[bit] for bit in NEAR],
            *[feature_near[bit] for bit in NEAR],
            *chunks_of(features_z),
        ),
    )
    output, grad_in = call(
        last_kernel,
        "output_and_grad_features",
        (shape(ROWS), shape(ROWS)),
        MAP_FLOPS,
        section_bit,
        (
            late,
            *[got_late[bit] for bit in NEAR],
            got_late[ZHI],
            hidden_far,
            local_first,
            diag_second,
            part_second,
        ),
    )
    hidden_near = after(*[hidden_near[bit] for bit in NEAR], bias_grad, output)[:5]
    diag_second_grad, part_second_grad, _ = weight_sums(
        "weights_second",
        section_bit,
        True,
        (
            late,
            hidden_rows,
            hidden_far,
            grad_out,
            gathered,
            *[got_late[bit] for bit in NEAR],
            *hidden_near,
            *chunks_of(grad_z),
        ),
    )
    return (
        output,
        grad_in,
        diag_first_grad,
        part_first_grad,
        bias_grad,
        diag_second_grad,
        part_second_grad,
    )


def solution(mesh):
    mesh = jax.sharding.Mesh(mesh.devices.reshape(N_DP, 4, 2, 8), ("dp", *FEAT))
    in_specs = (
        P("dp", FEAT),
        P(FEAT, None, None),
        P(None, FEAT, None, None),
        P(FEAT),
        P(FEAT, None, None),
        P(None, FEAT, None, None),
        P(),
        P("dp", FEAT),
    )
    out_specs = (
        P("dp", FEAT),
        P("dp", FEAT),
        P(FEAT, None, None),
        P(None, FEAT, None, None),
        P(FEAT),
        P(FEAT, None, None),
        P(None, FEAT, None, None),
    )
    return jax.shard_map(
        on_device, mesh=mesh, in_specs=in_specs, out_specs=out_specs, check_vma=False
    )
```

```python
import jax
import jax.numpy as jnp
from jax import lax
from jax.experimental import pallas as pl
from jax.experimental.pallas import tpu as pltpu
from jax.sharding import PartitionSpec as P

SECTIONS = 7
BS = 256
COLS = 512
ROWS = 256
REST = 768
N_DP = 4
N_FEAT = 64
CORE, X1, X2, ZHI, Y1, Y2 = range(6)
DEVICE_BITS = 6
FEAT = ("y", "z_hi", "x_core")
NEAR = (CORE, X1, X2, Y1, Y2)
START_ORDER = (X2, Y2, X1, Y1, ZHI, CORE)
SQRT_2_OVER_PI = 0.7978845608028654
CUBIC = 0.044715
VMEM_LIMIT = 60 * 1024 * 1024
BF16 = jnp.bfloat16
F32 = jnp.float32


def after(*values):
    return lax.optimization_barrier(values)


def from_partner(value, bit):
    pairs = [(source, source ^ (1 << bit)) for source in range(N_FEAT)]
    return lax.ppermute(value, FEAT, pairs)


def send(values):
    return {bit: from_partner(value, bit) for bit, value in values.items()}


def join(arrived, *values):
    tied = after(*arrived.values(), *values)
    return dict(zip(arrived, tied)), tied[len(arrived) :]


def tie(pair, *values):
    tied = after(*pair, *values)
    return tied[:2], tied[2:]


def along_z(value, step):
    pairs = []
    for dp in range(N_DP):
        for feat in range(N_FEAT):
            z_hi = (feat >> 3) & 1
            z = (z_hi * N_DP + dp + step) % (2 * N_DP)
            to_feat = (feat & ~8) | ((z // N_DP) << 3)
            pairs.append((dp * N_FEAT + feat, (z % N_DP) * N_FEAT + to_feat))
    return lax.ppermute(value, ("dp", *FEAT), pairs)


def both_ways(up, down):
    return along_z(up, 1), along_z(down, -1)


LINE = (
    ((1, 0), (1, 1), (1, 2)),
    ((1, 0), (1, 1), (0, 0)),
    ((1, 0), (0, 1), (0, 0)),
    ((0, 0), (0, 1), (0, 2)),
)
FAR = (
    ((0, 2), (0, 1), (0, 0)),
    ((0, 2), (0, 1), (1, 2)),
    ((0, 2), (1, 1), (1, 2)),
    ((1, 2), (1, 1), (1, 0)),
)


def dot(a, b):
    return jnp.dot(a, b, preferred_element_type=F32)


def dot_t(a, b):
    return lax.dot_general(a, b, (((1,), (1,)), ((), ())), preferred_element_type=F32)


def t_dot(a, b):
    return lax.dot_general(a, b, (((0,), (0,)), ((), ())), preferred_element_type=F32)


def sections_of(bits):
    return [
        sum(jnp.where(bits[section] == level, section, 0) for section in range(SECTIONS))
        for level in range(SECTIONS)
    ]


def half(block):
    return slice(block * BS, (block + 1) * BS)


def mix_block(order, own, others, diag, part, block):
    total = dot(own[0:ROWS, half(block)], diag[block])
    total = total + dot(own[0:ROWS, half(1 - block)], part[order[0], block])
    for bit in range(DEVICE_BITS):
        total = total + dot(others[bit][0:ROWS, half(block)], part[order[bit + 1], block])
    return total


def products(order, grad, diag, part, local, sent):
    for block in range(2):
        value = grad[:, half(block)]
        other = grad[:, half(1 - block)]
        local[:, half(block)] = dot_t(value, diag[block]) + dot_t(other, part[order[0], 1 - block])
        for bit in range(DEVICE_BITS):
            term = dot_t(value, part[order[bit + 1], block]).astype(BF16)
            sent[bit][sent[bit].shape[0] - ROWS :, half(block)] = term


def first_kernel(bits, features, grad, diag, part, local, *sent):
    order = sections_of(bits)
    for bit in range(DEVICE_BITS):
        sent[bit][0:ROWS] = features[...]
    products(order, grad, diag, part, local, sent)


def middle_kernel(bits, features, local_in, *refs):
    got, (diag, part, bias, late, local, *sent) = refs[:6], refs[6:]
    order = sections_of(bits)
    for block in range(2):
        pre = mix_block(order, features, got, diag, part, block)
        pre = pre + bias[half(block)].astype(F32)[None, :]
        tanh = jnp.tanh(SQRT_2_OVER_PI * (pre + CUBIC * pre * pre * pre))
        hidden = (0.5 * pre * (1.0 + tanh)).astype(BF16)
        late[0:ROWS, half(block)] = hidden
        for bit in NEAR:
            sent[bit][0:ROWS, half(block)] = hidden
        total = local_in[:, half(block)]
        for bit in range(DEVICE_BITS):
            total = total + got[bit][ROWS:, half(block)].astype(F32)
        slope = SQRT_2_OVER_PI * (1.0 + (3.0 * CUBIC) * pre * pre)
        gain = 0.5 * (1.0 + tanh) + 0.5 * pre * (1.0 - tanh * tanh) * slope
        late[ROWS : 2 * ROWS, half(block)] = (total * gain).astype(BF16)
    products(order, late.at[ROWS : 2 * ROWS], diag, part, local, sent)


def last_kernel(bits, hidden, *refs):
    order = sections_of(bits)
    got, got_far, far, (local, diag, part, out, grad_in) = refs[:5], refs[5], refs[6], refs[7:]
    others = dict(zip(NEAR, got))
    others[ZHI] = far
    for block in range(2):
        total = mix_block(order, hidden, others, diag, part, block)
        out[:, half(block)] = total.astype(BF16)
    total = local[...] + got_far[...].astype(F32)
    for ref in got:
        total = total + ref[ROWS:].astype(F32)
    grad_in[...] = total.astype(BF16)


def of_this_dp(body):
    for dp in range(N_DP):

        @pl.when(lax.axis_index("dp") == dp)
        def _():
            body(dp)


def rows_kernel(bits, *refs):
    chunks, out, sem = (refs[0:3], refs[3:6]), refs[6], refs[7]

    def copy(way, step, at):
        return pltpu.make_async_copy(
            chunks[way][step].at[pl.ds(0, ROWS)], out.at[pl.ds(at * ROWS, ROWS)], sem.at[at]
        )

    @of_this_dp
    def _(dp):
        for at, (way, step) in enumerate(LINE[dp]):
            copy(way, step, at).start()

    for at in range(3):
        copy(0, 0, at).wait()


def other_dp(dp, at):
    way, step = LINE[dp][at]
    return dp + 1 + step if way else dp - 1 - step


def gathered_row(dp, far, rows):
    z_hi = lax.axis_index("z_hi")
    if far:
        z_hi = 1 - z_hi
    return pl.multiple_of((z_hi * N_DP + dp) * rows, rows)


def hidden_rows_kernel(bits, gathered, rows, far, sem):
    def copy(row, out, at, order):
        return pltpu.make_async_copy(
            gathered.at[pl.ds(row, ROWS)], out.at[pl.ds(at * ROWS, ROWS)], sem.at[order]
        )

    @of_this_dp
    def _(dp):
        for at in range(3):
            copy(gathered_row(other_dp(dp, at), False, 2 * ROWS), rows, at, at).start()
        copy(gathered_row(dp, True, 2 * ROWS), far, 0, 3).start()

    for at in range(3):
        copy(0, rows, at, at).wait()
    copy(0, far, 0, 3).wait()


def weight_kernel(second, bits, *refs):
    order = sections_of(bits)
    own, own_rest, far, grad, gathered = refs[0:5]
    near, near_rest = refs[5:10], refs[10:15]
    chunks = (refs[15:18], refs[18:21])
    diag_out, part_out, bias_out, own_buf, far_buf, grad_buf, near_buf, sems = refs[21:]

    def copy(source, at, rows, target, to, sem):
        return pltpu.make_async_copy(
            source.at[pl.ds(at, rows)], target.at[pl.ds(to, rows)], sems.at[sem]
        )

    def grad_copy(at, source, row):
        return copy(source, row, ROWS, grad_buf, (at + 1) * ROWS, 1 + at)

    def far_copy(at, source, row):
        return copy(source, row, ROWS, far_buf, (at + 1) * ROWS, 7 + at)

    grad_copies = [copy(grad, 0 if second else ROWS, ROWS, grad_buf, 0, 0)]
    grad_copies += [grad_copy(at, gathered, 0) for at in range(3)]
    far_copies = [copy(far, 0, ROWS, far_buf, 0, 6)]
    far_copies += [far_copy(at, gathered, 0) for at in range(3)]
    own_copies = [
        copy(own, 0, ROWS, own_buf, 0, 4),
        copy(own_rest, 0, REST, own_buf, ROWS, 5),
    ]
    near_copies = []
    for at in range(5):
        buf = near_buf.at[at]
        near_copies.append(
            [
                copy(near[at], 0, ROWS, buf, 0, 10 + 2 * at),
                copy(near_rest[at], 0, REST, buf, ROWS, 11 + 2 * at),
            ]
        )
    grad_copies[0].start()

    @of_this_dp
    def _(dp):
        for at in range(3):
            other = other_dp(dp, at)
            if second:
                way, step = LINE[dp][at]
                source = chunks[way][step]
                grad_copy(at, source, source.shape[0] - ROWS).start()
                far_copy(at, gathered, gathered_row(other, True, 2 * ROWS)).start()
            else:
                row = gathered_row(other, False, 2 * ROWS)
                grad_copy(at, gathered, row + ROWS).start()
                way, step = FAR[dp][at]
                far_copy(at, chunks[way][step], 0).start()

    for item in (*own_copies, far_copies[0]):
        item.start()
    for pair in near_copies:
        for item in pair:
            item.start()
    for item in grad_copies:
        item.wait()
    for block in range(2):
        total = jnp.sum(grad_buf[:, half(block)].astype(F32), axis=0, keepdims=True)
        bias_out[half(block)] = total[0].astype(BF16)
    for item in own_copies:
        item.wait()
    for block in range(2):
        grads = grad_buf[:, half(block)]
        diag_out[block] = t_dot(own_buf[:, half(block)], grads).astype(BF16)
        part_out[order[0], block] = t_dot(own_buf[:, half(1 - block)], grads).astype(BF16)
    for item in far_copies:
        item.wait()
    for block in range(2):
        term = t_dot(far_buf[:, half(block)], grad_buf[:, half(block)])
        part_out[order[ZHI + 1], block] = term.astype(BF16)
    for at, bit in enumerate(NEAR):
        for item in near_copies[at]:
            item.wait()
        for block in range(2):
            term = t_dot(near_buf[at, :, half(block)], grad_buf[:, half(block)])
            part_out[order[bit + 1], block] = term.astype(BF16)


def shape(rows, dtype=BF16):
    return jax.ShapeDtypeStruct((rows, COLS), dtype)


def whole(value):
    zeros = (0,) * len(value.shape)
    return pl.BlockSpec(value.shape, lambda step: zeros)


HBM = pl.BlockSpec(memory_space=pl.ANY)
SCALARS = pl.BlockSpec(memory_space=pltpu.SMEM)
MAP_FLOPS = 2 * 16 * BS * BS * BS


def call(kernel, name, out_shape, flops, bits, args, fetch=True, scratch=(), outs=None):
    moved = sum(a.size * a.dtype.itemsize for a in (*args, *out_shape))
    return pl.pallas_call(
        kernel,
        grid=(1,),
        out_shape=out_shape,
        in_specs=[SCALARS] + [whole(value) if fetch else HBM for value in args],
        out_specs=outs or [whole(value) for value in out_shape],
        scratch_shapes=scratch,
        compiler_params=pltpu.CompilerParams(vmem_limit_bytes=VMEM_LIMIT),
        cost_estimate=pl.CostEstimate(flops=flops, bytes_accessed=moved, transcendentals=0),
        name=name,
    )(bits, *args)


def chunks_of(steps):
    return [item[0] for item in steps] + [item[1] for item in steps]


def rows_of_line(name, bits, steps):
    (rows,) = call(
        rows_kernel,
        name,
        (shape(REST),),
        0,
        bits,
        chunks_of(steps),
        fetch=False,
        scratch=[pltpu.SemaphoreType.DMA((3,))],
    )
    return rows


def weight_sums(name, bits, second, args):
    def kernel(*refs):
        weight_kernel(second, *refs)

    stacked = (N_DP * ROWS, COLS)
    return call(
        kernel,
        name,
        (
            jax.ShapeDtypeStruct((2, BS, BS), BF16),
            jax.ShapeDtypeStruct((SECTIONS, 2, BS, BS), BF16),
            jax.ShapeDtypeStruct((COLS,), BF16),
        ),
        N_DP * MAP_FLOPS,
        bits,
        args,
        fetch=False,
        scratch=[
            pltpu.VMEM(stacked, BF16),
            pltpu.VMEM(stacked, BF16),
            pltpu.VMEM(stacked, BF16),
            pltpu.VMEM((5, *stacked), BF16),
            pltpu.SemaphoreType.DMA((20,)),
        ],
    )


def on_device(
    features, diag_first, part_first, bias_first, diag_second, part_second, section_bit, grad_out
):
    bits = range(DEVICE_BITS)

    features_z = [both_ways(features, features)]
    local_second, *sent = call(
        first_kernel,
        "products_second",
        (shape(ROWS, F32), *[shape(2 * ROWS)] * 6),
        MAP_FLOPS,
        section_bit,
        (features, grad_out, diag_second, part_second),
    )
    *ends, local_second = after(*features_z[0], *sent, local_second)
    sent = ends[2:]
    got = send({bit: sent[bit] for bit in START_ORDER})
    up, down, *tied = after(*ends[:2], *[got[bit] for bit in bits])
    got = dict(zip(bits, tied))
    features_z[0] = (up, down)
    features_z.append(
        both_ways(*[jnp.concatenate([value, grad_out], axis=0) for value in (up, down)])
    )
    late, local_first, *sent = call(
        middle_kernel,
        "hidden_and_grad_pre",
        (shape(2 * ROWS), shape(ROWS, F32))
        + tuple(shape(ROWS if bit == ZHI else 2 * ROWS) for bit in bits),
        2 * MAP_FLOPS,
        section_bit,
        (
            features,
            local_second,
            *[got[bit] for bit in bits],
            diag_first,
            part_first,
            bias_first,
        ),
    )
    up, down, late = after(*features_z[1], late)
    features_z[1] = (up, down)
    gathered = lax.all_gather(late, ("z_hi", "dp"), axis=0, tiled=True)
    features_z.append(both_ways(up, down))
    got_late = send({bit: sent[bit] for bit in (X2, Y2, X1)})
    features_z[2], (sent[Y1], sent[CORE]) = tie(features_z[2], sent[Y1], sent[CORE])
    got_late.update(send({Y1: sent[Y1], CORE: sent[CORE]}))
    feature_rows = rows_of_line("feature_rows", section_bit, features_z)
    feature_rows, got_late[X2], got_late[Y2] = after(feature_rows, got_late[X2], got_late[Y2])
    feature_near = send({X2: feature_rows, Y2: feature_rows})
    got_late, (feature_rows,) = join(got_late, feature_rows)
    feature_near.update(send({X1: feature_rows, Y1: feature_rows, CORE: feature_rows}))
    gathered, feature_near[X2], feature_near[Y2] = after(
        gathered, feature_near[X2], feature_near[Y2]
    )
    hidden_rows, hidden_far = call(
        hidden_rows_kernel,
        "hidden_rows",
        (shape(REST), shape(ROWS)),
        0,
        section_bit,
        (gathered,),
        fetch=False,
        scratch=[pltpu.SemaphoreType.DMA((4,))],
    )
    hidden_near = send({X2: hidden_rows, Y2: hidden_rows})
    feature_near, (hidden_rows,) = join(feature_near, hidden_rows)
    hidden_near.update(send({X1: hidden_rows, Y1: hidden_rows, CORE: hidden_rows}))
    far_product, hidden_near[CORE] = after(sent[ZHI], hidden_near[CORE])
    got_late[ZHI] = from_partner(far_product, ZHI)
    diag_first_grad, part_first_grad, bias_grad = weight_sums(
        "weights_first",
        section_bit,
        False,
        (
            features,
            feature_rows,
            got[ZHI],
            late,
            gathered,
            *[got[bit] for bit in NEAR],
            *[feature_near[bit] for bit in NEAR],
            *chunks_of(features_z),
        ),
    )
    up, down, bias_grad = after(*[value[ROWS:] for value in features_z[2]], bias_grad)
    grad_z = [*features_z[1:], both_ways(up, down)]
    output, grad_in = call(
        last_kernel,
        "output_and_grad_features",
        (shape(ROWS), shape(ROWS)),
        MAP_FLOPS,
        section_bit,
        (
            late,
            *[got_late[bit] for bit in NEAR],
            got_late[ZHI],
            hidden_far,
            local_first,
            diag_second,
            part_second,
        ),
    )
    hidden_near = after(*[hidden_near[bit] for bit in NEAR], bias_grad, output)[:5]
    diag_second_grad, part_second_grad, _ = weight_sums(
        "weights_second",
        section_bit,
        True,
        (
            late,
            hidden_rows,
            hidden_far,
            grad_out,
            gathered,
            *[got_late[bit] for bit in NEAR],
            *hidden_near,
            *chunks_of(grad_z),
        ),
    )
    return (
        output,
        grad_in,
        diag_first_grad,
        part_first_grad,
        bias_grad,
        diag_second_grad,
        part_second_grad,
    )


def solution(mesh):
    mesh = jax.sharding.Mesh(mesh.devices.reshape(N_DP, 4, 2, 8), ("dp", *FEAT))
    in_specs = (
        P("dp", FEAT),
        P(FEAT, None, None),
        P(None, FEAT, None, None),
        P(FEAT),
        P(FEAT, None, None),
        P(None, FEAT, None, None),
        P(),
        P("dp", FEAT),
    )
    out_specs = (
        P("dp", FEAT),
        P("dp", FEAT),
        P(FEAT, None, None),
        P(None, FEAT, None, None),
        P(FEAT),
        P(FEAT, None, None),
        P(None, FEAT, None, None),
    )
    return jax.shard_map(
        on_device, mesh=mesh, in_specs=in_specs, out_specs=out_specs, check_vma=False
    )
```

```python
import jax
import jax.numpy as jnp
from jax import lax
from jax.experimental import pallas as pl
from jax.experimental.pallas import tpu as pltpu
from jax.sharding import PartitionSpec as P

SECTIONS = 7
BS = 256
COLS = 512
ROWS = 256
REST = 768
N_DP = 4
N_FEAT = 64
CORE, X1, X2, ZHI, Y1, Y2 = range(6)
DEVICE_BITS = 6
FEAT = ("y", "z_hi", "x_core")
NEAR = (CORE, X1, X2, Y1, Y2)
START_ORDER = (X2, Y2, X1, Y1, ZHI, CORE)
SQRT_2_OVER_PI = 0.7978845608028654
CUBIC = 0.044715
VMEM_LIMIT = 60 * 1024 * 1024
BF16 = jnp.bfloat16
F32 = jnp.float32


def after(*values):
    return lax.optimization_barrier(values)


def from_partner(value, bit):
    pairs = [(source, source ^ (1 << bit)) for source in range(N_FEAT)]
    return lax.ppermute(value, FEAT, pairs)


def send(values):
    return {bit: from_partner(value, bit) for bit, value in values.items()}


def join(arrived, *values):
    tied = after(*arrived.values(), *values)
    return dict(zip(arrived, tied)), tied[len(arrived) :]


def tie(pair, *values):
    tied = after(*pair, *values)
    return tied[:2], tied[2:]


def along_z(value, step):
    pairs = []
    for dp in range(N_DP):
        for feat in range(N_FEAT):
            z_hi = (feat >> 3) & 1
            z = (z_hi * N_DP + dp + step) % (2 * N_DP)
            to_feat = (feat & ~8) | ((z // N_DP) << 3)
            pairs.append((dp * N_FEAT + feat, (z % N_DP) * N_FEAT + to_feat))
    return lax.ppermute(value, ("dp", *FEAT), pairs)


def both_ways(up, down):
    return along_z(up, 1), along_z(down, -1)


LINE = (
    ((1, 0), (1, 1), (1, 2)),
    ((1, 0), (1, 1), (0, 0)),
    ((1, 0), (0, 1), (0, 0)),
    ((0, 0), (0, 1), (0, 2)),
)
FAR = (
    ((0, 2), (0, 1), (0, 0)),
    ((0, 2), (0, 1), (1, 2)),
    ((0, 2), (1, 1), (1, 2)),
    ((1, 2), (1, 1), (1, 0)),
)


def dot(a, b):
    return jnp.dot(a, b, preferred_element_type=F32)


def dot_t(a, b):
    return lax.dot_general(a, b, (((1,), (1,)), ((), ())), preferred_element_type=F32)


def t_dot(a, b):
    return lax.dot_general(a, b, (((0,), (0,)), ((), ())), preferred_element_type=F32)


def sections_of(bits):
    return [
        sum(jnp.where(bits[section] == level, section, 0) for section in range(SECTIONS))
        for level in range(SECTIONS)
    ]


def half(block):
    return slice(block * BS, (block + 1) * BS)


def mix_block(order, own, others, diag, part, block):
    total = dot(own[0:ROWS, half(block)], diag[block])
    total = total + dot(own[0:ROWS, half(1 - block)], part[order[0], block])
    for bit in range(DEVICE_BITS):
        total = total + dot(others[bit][0:ROWS, half(block)], part[order[bit + 1], block])
    return total


def products(order, grad, diag, part, local, sent):
    for block in range(2):
        value = grad[:, half(block)]
        other = grad[:, half(1 - block)]
        local[:, half(block)] = dot_t(value, diag[block]) + dot_t(other, part[order[0], 1 - block])
        for bit in range(DEVICE_BITS):
            term = dot_t(value, part[order[bit + 1], block]).astype(BF16)
            sent[bit][sent[bit].shape[0] - ROWS :, half(block)] = term


def first_kernel(bits, features, grad, diag, part, local, *sent):
    order = sections_of(bits)
    for bit in range(DEVICE_BITS):
        sent[bit][0:ROWS] = features[...]
    products(order, grad, diag, part, local, sent)


def middle_kernel(bits, features, local_in, *refs):
    got, (diag, part, bias, late, local, *sent) = refs[:6], refs[6:]
    order = sections_of(bits)
    for block in range(2):
        pre = mix_block(order, features, got, diag, part, block)
        pre = pre + bias[half(block)].astype(F32)[None, :]
        tanh = jnp.tanh(SQRT_2_OVER_PI * (pre + CUBIC * pre * pre * pre))
        hidden = (0.5 * pre * (1.0 + tanh)).astype(BF16)
        late[0:ROWS, half(block)] = hidden
        for bit in NEAR:
            sent[bit][0:ROWS, half(block)] = hidden
        total = local_in[:, half(block)]
        for bit in range(DEVICE_BITS):
            total = total + got[bit][ROWS:, half(block)].astype(F32)
        slope = SQRT_2_OVER_PI * (1.0 + (3.0 * CUBIC) * pre * pre)
        gain = 0.5 * (1.0 + tanh) + 0.5 * pre * (1.0 - tanh * tanh) * slope
        late[ROWS : 2 * ROWS, half(block)] = (total * gain).astype(BF16)
    products(order, late.at[ROWS : 2 * ROWS], diag, part, local, sent)


def last_kernel(bits, hidden, *refs):
    order = sections_of(bits)
    got, got_far, far, (local, diag, part, out, grad_in) = refs[:5], refs[5], refs[6], refs[7:]
    others = dict(zip(NEAR, got))
    others[ZHI] = far
    for block in range(2):
        total = mix_block(order, hidden, others, diag, part, block)
        out[:, half(block)] = total.astype(BF16)
    total = local[...] + got_far[...].astype(F32)
    for ref in got:
        total = total + ref[ROWS:].astype(F32)
    grad_in[...] = total.astype(BF16)


def of_this_dp(body):
    for dp in range(N_DP):

        @pl.when(lax.axis_index("dp") == dp)
        def _():
            body(dp)


def rows_kernel(bits, *refs):
    chunks, out, sem = (refs[0:3], refs[3:6]), refs[6], refs[7]

    def copy(way, step, at):
        return pltpu.make_async_copy(
            chunks[way][step].at[pl.ds(0, ROWS)], out.at[pl.ds(at * ROWS, ROWS)], sem.at[at]
        )

    @of_this_dp
    def _(dp):
        for at, (way, step) in enumerate(LINE[dp]):
            copy(way, step, at).start()

    for at in range(3):
        copy(0, 0, at).wait()


def other_dp(dp, at):
    way, step = LINE[dp][at]
    return dp + 1 + step if way else dp - 1 - step


def gathered_row(dp, far, rows):
    z_hi = lax.axis_index("z_hi")
    if far:
        z_hi = 1 - z_hi
    return pl.multiple_of((z_hi * N_DP + dp) * rows, rows)


def hidden_rows_kernel(bits, gathered, rows, far, sem):
    def copy(row, out, at, order):
        return pltpu.make_async_copy(
            gathered.at[pl.ds(row, ROWS)], out.at[pl.ds(at * ROWS, ROWS)], sem.at[order]
        )

    @of_this_dp
    def _(dp):
        for at in range(3):
            copy(gathered_row(other_dp(dp, at), False, 2 * ROWS), rows, at, at).start()
        copy(gathered_row(dp, True, 2 * ROWS), far, 0, 3).start()

    for at in range(3):
        copy(0, rows, at, at).wait()
    copy(0, far, 0, 3).wait()


def weight_kernel(second, bits, *refs):
    order = sections_of(bits)
    own, own_rest, far, grad, gathered = refs[0:5]
    near, near_rest = refs[5:10], refs[10:15]
    chunks = (refs[15:18], refs[18:21])
    diag_out, part_out, bias_out, own_buf, far_buf, grad_buf, near_buf, sems = refs[21:]

    def copy(source, at, rows, target, to, sem):
        return pltpu.make_async_copy(
            source.at[pl.ds(at, rows)], target.at[pl.ds(to, rows)], sems.at[sem]
        )

    def grad_copy(at, source, row):
        return copy(source, row, ROWS, grad_buf, (at + 1) * ROWS, 1 + at)

    def far_copy(at, source, row):
        return copy(source, row, ROWS, far_buf, (at + 1) * ROWS, 7 + at)

    grad_copies = [copy(grad, 0 if second else ROWS, ROWS, grad_buf, 0, 0)]
    grad_copies += [grad_copy(at, gathered, 0) for at in range(3)]
    far_copies = [copy(far, 0, ROWS, far_buf, 0, 6)]
    far_copies += [far_copy(at, gathered, 0) for at in range(3)]
    own_copies = [
        copy(own, 0, ROWS, own_buf, 0, 4),
        copy(own_rest, 0, REST, own_buf, ROWS, 5),
    ]
    near_copies = []
    for at in range(5):
        buf = near_buf.at[at]
        near_copies.append(
            [
                copy(near[at], 0, ROWS, buf, 0, 10 + 2 * at),
                copy(near_rest[at], 0, REST, buf, ROWS, 11 + 2 * at),
            ]
        )
    grad_copies[0].start()

    @of_this_dp
    def _(dp):
        for at in range(3):
            other = other_dp(dp, at)
            if second:
                way, step = LINE[dp][at]
                source = chunks[way][step]
                grad_copy(at, source, source.shape[0] - ROWS).start()
                far_copy(at, gathered, gathered_row(other, True, 2 * ROWS)).start()
            else:
                row = gathered_row(other, False, 2 * ROWS)
                grad_copy(at, gathered, row + ROWS).start()
                way, step = FAR[dp][at]
                far_copy(at, chunks[way][step], 0).start()

    for item in (*own_copies, far_copies[0]):
        item.start()
    for pair in near_copies:
        for item in pair:
            item.start()
    for item in grad_copies:
        item.wait()
    for block in range(2):
        total = jnp.sum(grad_buf[:, half(block)].astype(F32), axis=0, keepdims=True)
        bias_out[half(block)] = total[0].astype(BF16)
    for item in own_copies:
        item.wait()
    for block in range(2):
        grads = grad_buf[:, half(block)]
        diag_out[block] = t_dot(own_buf[:, half(block)], grads).astype(BF16)
        part_out[order[0], block] = t_dot(own_buf[:, half(1 - block)], grads).astype(BF16)
    for item in far_copies:
        item.wait()
    for block in range(2):
        term = t_dot(far_buf[:, half(block)], grad_buf[:, half(block)])
        part_out[order[ZHI + 1], block] = term.astype(BF16)
    for at, bit in enumerate(NEAR):
        for item in near_copies[at]:
            item.wait()
        for block in range(2):
            term = t_dot(near_buf[at, :, half(block)], grad_buf[:, half(block)])
            part_out[order[bit + 1], block] = term.astype(BF16)


def shape(rows, dtype=BF16):
    return jax.ShapeDtypeStruct((rows, COLS), dtype)


def whole(value):
    zeros = (0,) * len(value.shape)
    return pl.BlockSpec(value.shape, lambda step: zeros)


HBM = pl.BlockSpec(memory_space=pl.ANY)
SCALARS = pl.BlockSpec(memory_space=pltpu.SMEM)
MAP_FLOPS = 2 * 16 * BS * BS * BS


def call(kernel, name, out_shape, flops, bits, args, fetch=True, scratch=(), outs=None):
    moved = sum(a.size * a.dtype.itemsize for a in (*args, *out_shape))
    return pl.pallas_call(
        kernel,
        grid=(1,),
        out_shape=out_shape,
        in_specs=[SCALARS] + [whole(value) if fetch else HBM for value in args],
        out_specs=outs or [whole(value) for value in out_shape],
        scratch_shapes=scratch,
        compiler_params=pltpu.CompilerParams(vmem_limit_bytes=VMEM_LIMIT),
        cost_estimate=pl.CostEstimate(flops=flops, bytes_accessed=moved, transcendentals=0),
        name=name,
    )(bits, *args)


def chunks_of(steps):
    return [item[0] for item in steps] + [item[1] for item in steps]


def rows_of_line(name, bits, steps):
    (rows,) = call(
        rows_kernel,
        name,
        (shape(REST),),
        0,
        bits,
        chunks_of(steps),
        fetch=False,
        scratch=[pltpu.SemaphoreType.DMA((3,))],
    )
    return rows


def weight_sums(name, bits, second, args):
    def kernel(*refs):
        weight_kernel(second, *refs)

    stacked = (N_DP * ROWS, COLS)
    return call(
        kernel,
        name,
        (
            jax.ShapeDtypeStruct((2, BS, BS), BF16),
            jax.ShapeDtypeStruct((SECTIONS, 2, BS, BS), BF16),
            jax.ShapeDtypeStruct((COLS,), BF16),
        ),
        N_DP * MAP_FLOPS,
        bits,
        args,
        fetch=False,
        scratch=[
            pltpu.VMEM(stacked, BF16),
            pltpu.VMEM(stacked, BF16),
            pltpu.VMEM(stacked, BF16),
            pltpu.VMEM((5, *stacked), BF16),
            pltpu.SemaphoreType.DMA((20,)),
        ],
    )


def on_device(
    features, diag_first, part_first, bias_first, diag_second, part_second, section_bit, grad_out
):
    bits = range(DEVICE_BITS)

    features_z = [both_ways(features, features)]
    local_second, *sent = call(
        first_kernel,
        "products_second",
        (shape(ROWS, F32), *[shape(2 * ROWS)] * 6),
        MAP_FLOPS,
        section_bit,
        (features, grad_out, diag_second, part_second),
    )
    *ends, local_second = after(*features_z[0], *sent, local_second)
    sent = ends[2:]
    got = send({bit: sent[bit] for bit in START_ORDER})
    up, down, *tied = after(*ends[:2], *[got[bit] for bit in bits])
    got = dict(zip(bits, tied))
    features_z[0] = (up, down)
    features_z.append(both_ways(up, down))
    late, local_first, *sent = call(
        middle_kernel,
        "hidden_and_grad_pre",
        (shape(2 * ROWS), shape(ROWS, F32))
        + tuple(shape(ROWS if bit == ZHI else 2 * ROWS) for bit in bits),
        2 * MAP_FLOPS,
        section_bit,
        (
            features,
            local_second,
            *[got[bit] for bit in bits],
            diag_first,
            part_first,
            bias_first,
        ),
    )
    up, down, late = after(*features_z[1], late)
    features_z[1] = (up, down)
    gathered = lax.all_gather(late, ("z_hi", "dp"), axis=0, tiled=True)
    features_z.append(
        both_ways(*[jnp.concatenate([value, grad_out], axis=0) for value in (up, down)])
    )
    got_late = send({bit: sent[bit] for bit in (X2, Y2, X1)})
    features_z[2], (sent[Y1], sent[CORE]) = tie(features_z[2], sent[Y1], sent[CORE])
    got_late.update(send({Y1: sent[Y1], CORE: sent[CORE]}))
    feature_rows = rows_of_line("feature_rows", section_bit, features_z)
    feature_rows, got_late[X2], got_late[Y2] = after(feature_rows, got_late[X2], got_late[Y2])
    feature_near = send({X2: feature_rows, Y2: feature_rows})
    got_late, (feature_rows,) = join(got_late, feature_rows)
    feature_near.update(send({X1: feature_rows, Y1: feature_rows, CORE: feature_rows}))
    gathered, feature_near[X2], feature_near[Y2] = after(
        gathered, feature_near[X2], feature_near[Y2]
    )
    hidden_rows, hidden_far = call(
        hidden_rows_kernel,
        "hidden_rows",
        (shape(REST), shape(ROWS)),
        0,
        section_bit,
        (gathered,),
        fetch=False,
        scratch=[pltpu.SemaphoreType.DMA((4,))],
    )
    hidden_near = send({X2: hidden_rows, Y2: hidden_rows})
    feature_near, (hidden_rows,) = join(feature_near, hidden_rows)
    hidden_near.update(send({X1: hidden_rows, Y1: hidden_rows, CORE: hidden_rows}))
    far_product, hidden_near[CORE] = after(sent[ZHI], hidden_near[CORE])
    got_late[ZHI] = from_partner(far_product, ZHI)
    diag_first_grad, part_first_grad, bias_grad = weight_sums(
        "weights_first",
        section_bit,
        False,
        (
            features,
            feature_rows,
            got[ZHI],
            late,
            gathered,
            *[got[bit] for bit in NEAR],
            *[feature_near[bit] for bit in NEAR],
            *chunks_of(features_z),
        ),
    )
    up, down, bias_grad = after(*[value[ROWS:] for value in features_z[2]], bias_grad)
    grad_z = [features_z[2], both_ways(up, down)]
    grad_z.append(both_ways(*grad_z[1]))
    output, grad_in = call(
        last_kernel,
        "output_and_grad_features",
        (shape(ROWS), shape(ROWS)),
        MAP_FLOPS,
        section_bit,
        (
            late,
            *[got_late[bit] for bit in NEAR],
            got_late[ZHI],
            hidden_far,
            local_first,
            diag_second,
            part_second,
        ),
    )
    hidden_near = after(*[hidden_near[bit] for bit in NEAR], bias_grad, output)[:5]
    diag_second_grad, part_second_grad, _ = weight_sums(
        "weights_second",
        section_bit,
        True,
        (
            late,
            hidden_rows,
            hidden_far,
            grad_out,
            gathered,
            *[got_late[bit] for bit in NEAR],
            *hidden_near,
            *chunks_of(grad_z),
        ),
    )
    return (
        output,
        grad_in,
        diag_first_grad,
        part_first_grad,
        bias_grad,
        diag_second_grad,
        part_second_grad,
    )


def solution(mesh):
    mesh = jax.sharding.Mesh(mesh.devices.reshape(N_DP, 4, 2, 8), ("dp", *FEAT))
    in_specs = (
        P("dp", FEAT),
        P(FEAT, None, None),
        P(None, FEAT, None, None),
        P(FEAT),
        P(FEAT, None, None),
        P(None, FEAT, None, None),
        P(),
        P("dp", FEAT),
    )
    out_specs = (
        P("dp", FEAT),
        P("dp", FEAT),
        P(FEAT, None, None),
        P(None, FEAT, None, None),
        P(FEAT),
        P(FEAT, None, None),
        P(None, FEAT, None, None),
    )
    return jax.shard_map(
        on_device, mesh=mesh, in_specs=in_specs, out_specs=out_specs, check_vma=False
    )
```
